32 devices in a mesh: parts: 2 (over x), egroup: 8 (over z, y), inner: 2 (over core).
Axes of the slice: x: 2, y: 2, z: 4, core: 2. Of those that a mesh axis runs over, the one named last changes fastest.
Arguments:
- hidden_in: bfloat16 [4096, 3584], P(('parts', 'egroup', 'inner')), parts along dimension 0, may hold values from -6 to 6
- grad_out: bfloat16 [4096, 3584], P(('parts', 'egroup', 'inner')), parts along dimension 0, may hold values from -6 to 6
- gate_values: bfloat16 [4096, 2], P(('parts', 'egroup', 'inner')), parts along dimension 0, may hold values from 0.099609375 to 1
- expert_ids: int32 [4096, 2], P(('parts', 'egroup', 'inner')), parts along dimension 0, may hold values from 0 to 7, all different within a row; in each aligned block of 128 rows (0 to 127, 128 to 255, ...) at most 48 rows name the same one
- w_gate: bfloat16 [8, 3584, 1024], P('egroup', None, 'inner'), may hold values from -0.09375 to 0.09375
- w_up: bfloat16 [8, 3584, 1024], P('egroup', None, 'inner'), may hold values from -0.09375 to 0.09375
- w_down: bfloat16 [8, 1024, 3584], P('egroup', 'inner'), may hold values from -0.1875 to 0.1875
Outputs:
- grad_x: bfloat16 [4096, 3584], P(('parts', 'egroup', 'inner')), parts along dimension 0
- grad_gates: bfloat16 [4096, 2], P(('parts', 'egroup', 'inner')), parts along dimension 0
- grad_w_gate: bfloat16 [16, 3584, 1024], P(('parts', 'egroup'), None, 'inner'), parts along dimension 0
- grad_w_up: bfloat16 [16, 3584, 1024], P(('parts', 'egroup'), None, 'inner'), parts along dimension 0
- grad_w_down: bfloat16 [16, 1024, 3584], P(('parts', 'egroup'), 'inner'), parts along dimension 0
The draws below stay inside these ranges and needn't reach their ends.
There are 2 independent parts, one for each index of `parts`. The reference program is written for one: setup_inputs(seed, part) draws one part's arguments, and reference() takes and returns one part's arrays. A program takes and returns all parts, laid end to end along the dimension named above; an argument that names none is the same for every part. Nothing has to cross between parts.
Inputs may be any that keep to these rules, and one draw needn't show every extreme that they name: `expert_ids`: each row names 2 different experts. Among the 128 rows of one device no expert is named more than 48 times, and in every draw some device names some expert exactly 48 times.
All inputs are finite; a program needn't handle non-finite values.
Results may differ from the reference program's by a relative error of at most 0.011.
Values may be sent and summed in bfloat16 or wider, within the bound.
A program may use at most 128 MiB of HBM per device.

```python
import math
import jax
import jax.numpy as jnp
import numpy as np
from jax import lax

D = 3584
HID = 1024
TOPK = 2
TOK_DEV = 128
EXPERTS = 8
TOKENS = 2048
HID_DEV = 512
CAP = 48
N_EGROUP = 8
N_INNER = 2


def block_scale(own_key, extent, shards, low, top_value):
    level, own = 1.0, jax.random.fold_in(own_key, 6)
    for position, blocks in shards:
        steps = jnp.exp(jax.random.uniform(jax.random.fold_in(own, position), (blocks,), jnp.float32, low / len(shards), top_value / len(shards)))
        level = level * jnp.repeat(steps, extent[position] // blocks).reshape([-1 if axis == position else 1 for axis in range(len(extent))])
    return level


def assign_block(stream_key, own, number, rows, amount, top, reach, skew):
    ranking = jax.random.permutation(stream_key, amount)
    crowded, ordinary = load_shares(amount, rows * top, reach, skew, True), load_shares(amount, rows * top, reach, skew, False)
    places = jnp.arange(amount)

    def named(tallies, turn):
        used = int((tallies > 0).sum())
        fixed = max(1, used // 4)
        passed = fixed + (places - fixed + turn * (used - fixed)) % max(1, amount - fixed)
        return jnp.zeros((amount,), jnp.int32).at[ranking[jnp.where(places < fixed, places, passed)]].set(jnp.asarray(tallies, jnp.int32))

    tallies = jnp.where(number % 4 == 0, named(crowded, number // 4), named(ordinary, number - number // 4 - 1))
    mixed = jax.random.permutation(jax.random.fold_in(own, 3), amount)
    donor, sink = mixed[0:amount // 2 * 2:2], mixed[1:amount // 2 * 2:2]
    room = jnp.minimum(tallies[donor] - 1, reach - tallies[sink]) // 2
    room = jnp.where((donor == ranking[0]) | (sink == ranking[0]) | (tallies[sink] == 0), 0, jnp.maximum(room, 0))
    passed = jax.random.randint(jax.random.fold_in(own, 4), (amount // 2,), 0, 1 << 20) % (room + 1)
    tallies = tallies.at[donor].add(-passed).at[sink].add(passed)
    labels = jnp.searchsorted(jnp.cumsum(tallies), jnp.arange(rows * top), side="right").astype(jnp.int32)
    listing = labels.reshape(top, rows).T
    listing = listing[jax.random.permutation(jax.random.fold_in(own, 1), rows)]
    turn = jax.random.randint(jax.random.fold_in(own, 2), (rows, 1), 0, top)
    return jnp.take_along_axis(listing, (jnp.arange(top)[None, :] + turn) % top, axis=1)


def load_shares(number_of, total, limit, skew, full):
    loads = [(1 << 20) // math.isqrt(rank ** skew) + 1 for rank in range(1, number_of + 1)]
    largest = limit if full else min(limit, max(-(-total // number_of), total * loads[0] // sum(loads)))
    least = 1 if total - largest >= number_of - 1 else 0
    counts, surplus = [largest] + [least] * (number_of - 1), total - largest - least * (number_of - 1)
    while surplus > 0:
        free = [i for i in range(1, number_of) if counts[i] < largest] or [i for i in range(1, number_of) if counts[i] < limit]
        mass, budget = sum([loads[i] for i in free]), surplus
        for i in free:
            more = min(limit - counts[i], max(1, budget * loads[i] // mass), surplus)
            counts[i] = counts[i] + more
            surplus = surplus - more
    return np.array(counts)


def gaussian(key, shape, spread, reach, shards=(), kind=jnp.bfloat16):
    loudness = block_scale(key, shape, shards, -0.22, 0.18) if shards else 1.0
    drawn = jax.random.normal(key, shape, jnp.float32) * spread * loudness
    return jnp.minimum(jnp.maximum(drawn, -reach), reach).astype(kind)


def setup_inputs(seed: int = 0, part: int = 0) -> dict:
    streams_of = jax.random.split(jax.random.key(seed), 8)
    own_keys = jax.random.split(jax.random.fold_in(streams_of[7], part), 8)
    hidden_in = gaussian(own_keys[0], (TOKENS, D), 1.0, 6.0, ((0, 16),))
    grad_out = gaussian(own_keys[1], (TOKENS, D), 1.0, 6.0, ((0, 16),))
    gate_values = jnp.clip(0.099609375 + 0.9003906 * jax.random.uniform(own_keys[2], (TOKENS, TOPK), jnp.float32) ** block_scale(own_keys[2], (TOKENS, TOPK), ((0, 16),), -0.2, 0.2), 0.099609375, 1.0).astype(jnp.bfloat16)
    expert_ids_keys = jax.random.split(jax.random.fold_in(own_keys[3], 1), TOKENS // TOK_DEV)
    expert_ids_turns = jax.random.permutation(jax.random.fold_in(own_keys[3], 3), TOKENS // TOK_DEV)
    expert_ids = jax.vmap(lambda own, number: assign_block(jax.random.fold_in(own_keys[3], 2), own, number, TOK_DEV, EXPERTS, TOPK, CAP, 2))(expert_ids_keys, expert_ids_turns).reshape((TOKENS, TOPK))
    w_gate = gaussian(streams_of[4], (EXPERTS, D, HID), D ** -0.5, 0.09375, ((0, 8), (2, 2)))
    w_up = gaussian(streams_of[5], (EXPERTS, D, HID), D ** -0.5, 0.09375, ((0, 8), (2, 2)))
    w_down = gaussian(streams_of[6], (EXPERTS, HID, D), HID ** -0.5, 0.1875, ((0, 8), (1, 2)))
    return dict(hidden_in=hidden_in, grad_out=grad_out, gate_values=gate_values, expert_ids=expert_ids, w_gate=w_gate, w_up=w_up, w_down=w_down)


def slot_targets(expert_ids):
    devices = N_EGROUP * N_INNER
    per_device = expert_ids.reshape(devices, TOK_DEV * TOPK)
    onehot = (per_device[:, :, None] == jnp.arange(EXPERTS, dtype=jnp.int32)[None, None, :]).astype(jnp.int32)
    before = jnp.cumsum(onehot, axis=1) - onehot
    places = jnp.sum(before * onehot, axis=2)
    source = jnp.arange(devices, dtype=jnp.int32)[:, None] * CAP
    return (per_device * (devices * CAP) + source + places).reshape(-1).astype(jnp.int32)


def half_terms(in_rows, cotangent, gate_vals, gate_half, up_half, down_half):
    pre_gate = jnp.dot(in_rows, gate_half, preferred_element_type=jnp.float32)
    pre_up = jnp.dot(in_rows, up_half, preferred_element_type=jnp.float32)
    logistic = jax.nn.sigmoid(pre_gate)
    active = pre_gate * logistic
    hidden = (active * pre_up).astype(jnp.bfloat16)
    back_proj = jnp.dot(cotangent, down_half.T, preferred_element_type=jnp.float32)
    gate_col = gate_vals.astype(jnp.float32)[:, None]
    weighted = (gate_col * cotangent.astype(jnp.float32)).astype(jnp.bfloat16)
    grad_down = jnp.dot(hidden.T, weighted, preferred_element_type=jnp.float32)
    scaled = gate_col * back_proj
    grad_pre_gate = (scaled * pre_up * logistic * (1.0 + pre_gate * (1.0 - logistic))).astype(jnp.bfloat16)
    grad_pre_up = (scaled * active).astype(jnp.bfloat16)
    grad_gate = jnp.dot(in_rows.T, grad_pre_gate, preferred_element_type=jnp.float32)
    grad_up = jnp.dot(in_rows.T, grad_pre_up, preferred_element_type=jnp.float32)
    grad_rows = (jnp.dot(grad_pre_gate, gate_half.T, preferred_element_type=jnp.float32)
                 + jnp.dot(grad_pre_up, up_half.T, preferred_element_type=jnp.float32)).astype(jnp.bfloat16)
    grad_mix = jnp.sum(hidden.astype(jnp.float32) * back_proj, axis=1).astype(jnp.bfloat16)
    return grad_gate, grad_up, grad_down, grad_rows, grad_mix


def expert_terms(items):
    in_rows, cotangent, gate_vals, weight_gate, weight_up, weight_down = items
    results = []
    for half_index in range(N_INNER):
        lower = half_index * HID_DEV
        upper = lower + HID_DEV
        results.append(half_terms(in_rows, cotangent, gate_vals, weight_gate[:, lower:upper],
                                  weight_up[:, lower:upper], weight_down[lower:upper, :]))
    grad_gate = jnp.concatenate([item[0] for item in results], axis=1).astype(jnp.bfloat16)
    grad_up = jnp.concatenate([item[1] for item in results], axis=1).astype(jnp.bfloat16)
    grad_down = jnp.concatenate([item[2] for item in results], axis=0).astype(jnp.bfloat16)
    grad_rows = results[0][3].astype(jnp.float32)
    grad_mix = results[0][4].astype(jnp.float32)
    for item in results[1:]:
        grad_rows = grad_rows + item[3].astype(jnp.float32)
        grad_mix = grad_mix + item[4].astype(jnp.float32)
    return grad_gate, grad_up, grad_down, grad_rows.astype(jnp.bfloat16), grad_mix.astype(jnp.bfloat16)


def reference(hidden_in, grad_out, gate_values, expert_ids, w_gate, w_up, w_down):
    target = slot_targets(expert_ids)
    expert_rows = N_EGROUP * N_INNER * CAP
    all_slots = EXPERTS * expert_rows
    in_rows = jnp.zeros((all_slots, D), jnp.bfloat16).at[target].set(jnp.repeat(hidden_in, TOPK, axis=0))
    cotangent = jnp.zeros((all_slots, D), jnp.bfloat16).at[target].set(jnp.repeat(grad_out, TOPK, axis=0))
    gate_vals = jnp.zeros((all_slots,), jnp.bfloat16).at[target].set(gate_values.reshape(-1))
    grad_gate, grad_up, grad_down, grad_rows, grad_mix = lax.map(
        expert_terms,
        (in_rows.reshape(EXPERTS, expert_rows, D), cotangent.reshape(EXPERTS, expert_rows, D),
         gate_vals.reshape(EXPERTS, expert_rows), w_gate, w_up, w_down))
    picked = grad_rows.reshape(all_slots, D)[target].astype(jnp.float32)
    grad_x = jnp.sum(picked.reshape(TOKENS, TOPK, D), axis=1).astype(jnp.bfloat16)
    grad_gates = grad_mix.reshape(all_slots)[target].reshape(TOKENS, TOPK)
    return grad_x, grad_gates, grad_gate, grad_up, grad_down
```

```python
import functools

import jax
import jax.numpy as jnp
from jax import lax
from jax.experimental import pallas as pl
from jax.experimental.pallas import tpu as pltpu
from jax.sharding import PartitionSpec as P

F32 = jnp.float32
BF16 = jnp.bfloat16
LANES = 128
TILE = 512


def nt_dot(a, b):
    return lax.dot_general(a, b, (((1,), (1,)), ((), ())), preferred_element_type=F32)


def tn_dot(a, b):
    return lax.dot_general(a, b, (((0,), (0,)), ((), ())), preferred_element_type=F32)


def layer_kernel(
    n,
    capp,
    x_ref,
    cot_ref,
    gates_ref,
    ids_row_ref,
    ids_col_ref,
    wg_hbm,
    wu_hbm,
    wd_hbm,
    gx_ref,
    gg_ref,
    gwg_hbm,
    gwu_hbm,
    gwd_hbm,
    wg,
    wu,
    wd,
    sel,
    gate_sel,
    snd_x,
    snd_c,
    rx,
    rc,
    pg,
    pu,
    act,
    gpg,
    gpu,
    hbuf,
    sib,
    ret,
    w_sem,
    o_sem,
    xs,
    xr,
    cs,
    cr,
    fxs,
    fxr,
    fcs,
    fcr,
    hs,
    hr,
    rs,
    rr,
):
    g = lax.axis_index("egroup")
    i = lax.axis_index("inner")
    tok, dm = x_ref.shape
    rows = n * capp
    pair = 2 * capp
    tiles = dm // TILE
    bar = pltpu.get_barrier_semaphore()

    def signal(s, c):
        pl.semaphore_signal(bar, inc=1, device_id={"egroup": lax.rem(g + s, n)})
        return c

    lax.fori_loop(1, n, signal, 0)
    pl.semaphore_signal(bar, inc=1, device_id={"inner": 1 - i})
    w_copies = [
        pltpu.make_async_copy(wg_hbm, wg, w_sem.at[0]),
        pltpu.make_async_copy(wu_hbm, wu, w_sem.at[1]),
        pltpu.make_async_copy(wd_hbm, wd, w_sem.at[2]),
    ]
    for copy in w_copies:
        copy.start()

    def block(s):
        return pl.ds(pl.multiple_of(s * capp, 16), capp)

    def slot(s, j):
        return pl.ds(pl.multiple_of((s * 2 + j) * capp, 16), capp)

    def chunk(s):
        return pl.ds(pl.multiple_of(s * pair, 16), pair)

    def x_copy(s):
        return pltpu.make_async_remote_copy(
            src_ref=snd_x.at[block(s)],
            dst_ref=rx.at[slot(s, i)],
            send_sem=xs.at[s],
            recv_sem=xr.at[s],
            device_id={"egroup": lax.rem(g + s, n)},
        )

    def c_copy(s):
        return pltpu.make_async_remote_copy(
            src_ref=snd_c.at[block(s)],
            dst_ref=rc.at[slot(s, i)],
            send_sem=cs.at[s],
            recv_sem=cr.at[s],
            device_id={"egroup": lax.rem(g + s, n)},
        )

    def fx_copy(s, j):
        return pltpu.make_async_remote_copy(
            src_ref=rx.at[slot(s, j)],
            dst_ref=rx.at[slot(s, j)],
            send_sem=fxs.at[s],
            recv_sem=fxr.at[s],
            device_id={"inner": 1 - i},
        )

    def fc_copy(s, j):
        return pltpu.make_async_remote_copy(
            src_ref=rc.at[slot(s, j)],
            dst_ref=rc.at[slot(s, j)],
            send_sem=fcs.at[s],
            recv_sem=fcr.at[s],
            device_id={"inner": 1 - i},
        )

    def h_copy(s):
        return pltpu.make_async_remote_copy(
            src_ref=hbuf.at[slot(s, 1 - i)],
            dst_ref=sib.at[block(s)],
            send_sem=hs.at[s],
            recv_sem=hr.at[s],
            device_id={"inner": 1 - i},
        )

    def r_copy(s):
        return pltpu.make_async_remote_copy(
            src_ref=hbuf.at[slot(s, i)],
            dst_ref=ret.at[block(s)],
            send_sem=rs.at[s],
            recv_sem=rr.at[s],
            device_id={"egroup": lax.rem(g - s + n, n)},
        )

    pairs = 2 * tok
    ids_row, ids_col = ids_row_ref[...], ids_col_ref[...]
    qr = lax.broadcasted_iota(jnp.int32, (pairs, pairs), 0)
    qc = lax.broadcasted_iota(jnp.int32, (pairs, pairs), 1)
    order_r = jnp.where(qr >= tok, 2 * (qr - tok) + 1, 2 * qr)
    order_c = jnp.where(qc >= tok, 2 * (qc - tok) + 1, 2 * qc)
    same = ids_row == ids_col
    one, zero = jnp.float32(1), jnp.float32(0)
    slot_row = jnp.sum(jnp.where(same & (order_r < order_c), one, zero), axis=0, keepdims=True)
    slot_col = jnp.sum(jnp.where(same & (order_c < order_r), one, zero), axis=1, keepdims=True)

    def place(ids, slots):
        ahead = ids - g
        ahead = jnp.where(ahead < 0, ahead + n, ahead)
        return ahead.astype(F32) * capp + slots

    to_row = place(ids_row, slot_row)
    to_col = place(ids_col, slot_col)
    position = lax.broadcasted_iota(jnp.int32, (rows, pairs), 0).astype(F32)
    hot = jnp.where(position == to_row, one, zero)
    sel[...] = (hot[:, :tok] + hot[:, tok:]).astype(BF16)
    gate_sel[...] = jnp.dot(
        hot.astype(BF16), gates_ref[...], preferred_element_type=F32
    ).astype(BF16)

    pl.semaphore_wait(bar, n)

    def fill(s, src, dst, where):
        picks = sel[block(s), :]

        def tile(t, c):
            cols = pl.ds(pl.multiple_of(t * TILE, TILE), TILE)
            dst[where, cols] = jnp.dot(
                picks, src[:, cols], preferred_element_type=F32
            ).astype(BF16)
            return c

        lax.fori_loop(0, tiles, tile, 0)

    def start_x(s, c):
        fill(s, x_ref, snd_x, block(s))
        snd_x[block(s), dm:] = gate_sel[block(s), :]
        x_copy(s).start()
        return c

    lax.fori_loop(1, n, start_x, 0)
    fill(0, x_ref, rx, slot(0, i))
    rx[slot(0, i), dm:] = gate_sel[block(0), :]
    fx_copy(0, i).start()

    def fill_c(s, c):
        fill(s, cot_ref, snd_c, block(s))
        return c

    lax.fori_loop(1, n, fill_c, 0)
    fill(0, cot_ref, rc, slot(0, i))
    fc_copy(0, i).start()

    for copy in w_copies:
        copy.wait()

    def up_terms(s):
        fx_copy(s, 1 - i).wait_recv()
        inp = rx[chunk(s), :dm]
        pg[chunk(s), :] = jnp.dot(inp, wg[...], preferred_element_type=F32)
        pu[chunk(s), :] = jnp.dot(inp, wu[...], preferred_element_type=F32)

    def phase_x(s, c):
        x_copy(s).wait_recv()
        fx_copy(s, i).start()
        c_copy(s).start()
        up_terms(s - 1)
        return c

    lax.fori_loop(1, n, phase_x, 0)
    up_terms(n - 1)

    def down_terms(s):
        fc_copy(s, 1 - i).wait_recv()
        back = nt_dot(rc[chunk(s), :], wd[...])
        gate_col = rx[chunk(s), dm : dm + 1].astype(F32)
        pre_gate, pre_up = pg[chunk(s), :], pu[chunk(s), :]
        logistic = 1.0 / (1.0 + jnp.exp(-pre_gate))
        active = pre_gate * logistic
        hidden = (active * pre_up).astype(BF16)
        scaled = gate_col * back
        d_gate = (scaled * pre_up * logistic * (1.0 + pre_gate * (1.0 - logistic))).astype(BF16)
        d_up = (scaled * active).astype(BF16)
        act[chunk(s), :] = hidden
        gpg[chunk(s), :] = d_gate
        gpu[chunk(s), :] = d_up
        mix = jnp.sum(hidden.astype(F32) * back, axis=1, keepdims=True)
        hbuf[chunk(s), dm:] = jnp.broadcast_to(mix, (pair, LANES)).astype(BF16)

        def tile(t, c):
            cols = pl.ds(pl.multiple_of(t * TILE, TILE), TILE)
            hbuf[chunk(s), cols] = (
                nt_dot(gpg[chunk(s), :], wg[cols, :]) + nt_dot(gpu[chunk(s), :], wu[cols, :])
            ).astype(BF16)
            return c

        lax.fori_loop(0, tiles, tile, 0)
        h_copy(s).start()

    def add_halves(s):
        h_copy(s).wait_recv()
        return (hbuf[slot(s, i), :].astype(F32) + sib[block(s), :].astype(F32)).astype(BF16)

    def give_back(s):
        hbuf[slot(s, i), :] = add_halves(s)
        r_copy(s).start()

    c_copy(1).wait_recv()
    fc_copy(1, i).start()
    down_terms(0)

    def phase_c(s, c):
        @pl.when(s < n - 1)
        def _():
            c_copy(s + 1).wait_recv()
            fc_copy(s + 1, i).start()

        down_terms(s)

        @pl.when(s > 1)
        def _():
            give_back(s - 1)

        return c

    lax.fori_loop(1, n, phase_c, 0)
    give_back(n - 1)
    ret[block(0), :] = add_halves(0)

    def out_copies(t):
        cols = pl.ds(pl.multiple_of(t * TILE, TILE), TILE)
        return (
            pltpu.make_async_copy(wg.at[cols], gwg_hbm.at[cols], o_sem.at[0, t]),
            pltpu.make_async_copy(wu.at[cols], gwu_hbm.at[cols], o_sem.at[1, t]),
            pltpu.make_async_copy(wd.at[:, cols], gwd_hbm.at[:, cols], o_sem.at[2, t]),
        )

    def weight_grads(t, c):
        cols = pl.ds(pl.multiple_of(t * TILE, TILE), TILE)
        inp = rx[:, cols]
        wg[cols, :] = tn_dot(inp, gpg[...]).astype(BF16)
        wu[cols, :] = tn_dot(inp, gpu[...]).astype(BF16)
        gate_col = rx[:, dm : dm + 1].astype(F32)
        weighted = (gate_col * rc[:, cols].astype(F32)).astype(BF16)
        wd[:, cols] = tn_dot(act[...], weighted).astype(BF16)
        for copy in out_copies(t):
            copy.start()
        return c

    lax.fori_loop(0, tiles, weight_grads, 0)

    def finish(s, c):
        r_copy(s).wait_recv()
        return c

    lax.fori_loop(1, n, finish, 0)
    place_lane = lax.broadcasted_iota(jnp.int32, (pairs, rows), 1).astype(F32)
    hot_t = jnp.where(place_lane == to_col, one, zero)
    gg_ref[...] = jnp.dot(hot_t.astype(BF16), ret[:, dm:], preferred_element_type=F32).astype(BF16)
    sel_t = (hot_t[:tok, :] + hot_t[tok:, :]).astype(BF16)
    for t in range(tiles):
        cols = slice(t * TILE, (t + 1) * TILE)
        gx_ref[:, cols] = jnp.dot(sel_t, ret[:, cols], preferred_element_type=F32).astype(BF16)

    def drain(s, c):
        x_copy(s).wait_send()
        c_copy(s).wait_send()
        r_copy(s).wait_send()
        return c

    lax.fori_loop(1, n, drain, 0)

    def drain_pairs(s, c):
        fx_copy(s, i).wait_send()
        fc_copy(s, i).wait_send()
        h_copy(s).wait_send()
        return c

    lax.fori_loop(0, n, drain_pairs, 0)

    def drain_out(t, c):
        for copy in out_copies(t):
            copy.wait()
        return c

    lax.fori_loop(0, tiles, drain_out, 0)


def shards(hidden_in, grad_out, gate_values, expert_ids, w_gate, w_up, w_down):
    tok, dm = hidden_in.shape
    per_token = expert_ids.shape[1]
    n = lax.axis_size("egroup")
    hid = w_gate.shape[2]
    capacity = tok * per_token * 3 // (2 * n)
    capp = -(-capacity // 16) * 16
    rows = n * capp
    pairs = tok * per_token
    ids = expert_ids.T
    gates = jnp.broadcast_to(gate_values.T.reshape(pairs, 1), (pairs, LANES))
    wide = dm + LANES
    dma = pltpu.SemaphoreType.DMA
    vmem = pl.BlockSpec(memory_space=pltpu.VMEM)
    hbm = pl.BlockSpec(memory_space=pl.ANY)
    flops = 2 * 8 * 2 * rows * dm * hid
    gx, gg, gwg, gwu, gwd = pl.pallas_call(
        functools.partial(layer_kernel, n, capp),
        out_shape=(
            jax.ShapeDtypeStruct((tok, dm), BF16),
            jax.ShapeDtypeStruct((pairs, LANES), BF16),
            jax.ShapeDtypeStruct((dm, hid), BF16),
            jax.ShapeDtypeStruct((dm, hid), BF16),
            jax.ShapeDtypeStruct((hid, dm), BF16),
        ),
        in_specs=[vmem] * 5 + [hbm] * 3,
        out_specs=(vmem, vmem, hbm, hbm, hbm),
        scratch_shapes=[
            pltpu.VMEM((dm, hid), BF16),
            pltpu.VMEM((dm, hid), BF16),
            pltpu.VMEM((hid, dm), BF16),
            pltpu.VMEM((rows, tok), BF16),
            pltpu.VMEM((rows, LANES), BF16),
            pltpu.VMEM((rows, wide), BF16),
            pltpu.VMEM((rows, dm), BF16),
            pltpu.VMEM((2 * rows, wide), BF16),
            pltpu.VMEM((2 * rows, dm), BF16),
            pltpu.VMEM((2 * rows, hid), F32),
            pltpu.VMEM((2 * rows, hid), F32),
            pltpu.VMEM((2 * rows, hid), BF16),
            pltpu.VMEM((2 * rows, hid), BF16),
            pltpu.VMEM((2 * rows, hid), BF16),
            pltpu.VMEM((2 * rows, wide), BF16),
            pltpu.VMEM((rows, wide), BF16),
            pltpu.VMEM((rows, wide), BF16),
            dma((3,)),
            dma((3, dm // TILE)),
        ]
        + [dma((n,))] * 12,
        compiler_params=pltpu.CompilerParams(
            collective_id=0,
            has_side_effects=True,
            vmem_limit_bytes=63 * 1024 * 1024,
        ),
        cost_estimate=pl.CostEstimate(
            flops=flops, bytes_accessed=30_000_000, transcendentals=2 * rows * hid
        ),
        name="expert_layer",
    )(
        hidden_in,
        grad_out,
        gates,
        ids.reshape(1, pairs),
        ids.reshape(pairs, 1),
        w_gate[0],
        w_up[0],
        w_down[0],
    )
    grad_gates = gg[:, 0].reshape(per_token, tok).T
    return gx, grad_gates, gwg[None], gwu[None], gwd[None]


def solution(mesh):
    in_specs = (
        P(("parts", "egroup", "inner"), None),
        P(("parts", "egroup", "inner"), None),
        P(("parts", "egroup", "inner"), None),
        P(("parts", "egroup", "inner"), None),
        P("egroup", None, "inner"),
        P("egroup", None, "inner"),
        P("egroup", "inner", None),
    )
    out_specs = (
        P(("parts", "egroup", "inner"), None),
        P(("parts", "egroup", "inner"), None),
        P(("parts", "egroup"), None, "inner"),
        P(("parts", "egroup"), None, "inner"),
        P(("parts", "egroup"), "inner", None),
    )
    return jax.shard_map(shards, mesh=mesh, in_specs=in_specs, out_specs=out_specs, check_vma=False)
```

```python
import functools

import jax
import jax.numpy as jnp
from jax import lax
from jax.experimental import pallas as pl
from jax.experimental.pallas import tpu as pltpu
from jax.sharding import PartitionSpec as P

F32 = jnp.float32
BF16 = jnp.bfloat16
LANES = 128
TILE = 512


def nt_dot(a, b):
    return lax.dot_general(a, b, (((1,), (1,)), ((), ())), preferred_element_type=F32)


def tn_dot(a, b):
    return lax.dot_general(a, b, (((0,), (0,)), ((), ())), preferred_element_type=F32)


def layer_kernel(
    n,
    capp,
    x_ref,
    cot_ref,
    gates_ref,
    ids_ref,
    wg_hbm,
    wu_hbm,
    wd_hbm,
    gx_ref,
    gg_ref,
    gwg_hbm,
    gwu_hbm,
    gwd_hbm,
    wg,
    wu,
    wd,
    sel,
    gate_sel,
    snd_x,
    snd_c,
    rx,
    rc,
    pg,
    pu,
    act,
    gpg,
    gpu,
    hbuf,
    sib,
    ret,
    w_sem,
    o_sem,
    xs,
    xr,
    cs,
    cr,
    fxs,
    fxr,
    fcs,
    fcr,
    hs,
    hr,
    rs,
    rr,
):
    g = lax.axis_index("egroup")
    i = lax.axis_index("inner")
    tok, dm = x_ref.shape
    rows = n * capp
    pair = 2 * capp
    tiles = dm // TILE
    bar = pltpu.get_barrier_semaphore()

    def partner(s):
        far, total, bit = s, 0, 1
        while bit < n:
            total = total + lax.rem(lax.div(g, bit) + lax.div(far, bit), 2) * bit
            bit *= 2
        return total

    def signal(s, c):
        pl.semaphore_signal(bar, inc=1, device_id={"egroup": partner(s)})
        return c

    lax.fori_loop(1, n, signal, 0)
    pl.semaphore_signal(bar, inc=1, device_id={"inner": 1 - i})
    w_copies = [
        pltpu.make_async_copy(wg_hbm, wg, w_sem.at[0]),
        pltpu.make_async_copy(wu_hbm, wu, w_sem.at[1]),
        pltpu.make_async_copy(wd_hbm, wd, w_sem.at[2]),
    ]
    for copy in w_copies:
        copy.start()

    def block(s):
        return pl.ds(pl.multiple_of(s * capp, 16), capp)

    def slot(s, j):
        return pl.ds(pl.multiple_of((s * 2 + j) * capp, 16), capp)

    def chunk(s):
        return pl.ds(pl.multiple_of(s * pair, 16), pair)

    def x_copy(s):
        return pltpu.make_async_remote_copy(
            src_ref=snd_x.at[block(s)],
            dst_ref=rx.at[slot(s, i)],
            send_sem=xs.at[s],
            recv_sem=xr.at[s],
            device_id={"egroup": partner(s)},
        )

    def c_copy(s):
        return pltpu.make_async_remote_copy(
            src_ref=snd_c.at[block(s)],
            dst_ref=rc.at[slot(s, i)],
            send_sem=cs.at[s],
            recv_sem=cr.at[s],
            device_id={"egroup": partner(s)},
        )

    def fx_copy(s, j):
        return pltpu.make_async_remote_copy(
            src_ref=rx.at[slot(s, j)],
            dst_ref=rx.at[slot(s, j)],
            send_sem=fxs.at[s],
            recv_sem=fxr.at[s],
            device_id={"inner": 1 - i},
        )

    def fc_copy(s, j):
        return pltpu.make_async_remote_copy(
            src_ref=rc.at[slot(s, j)],
            dst_ref=rc.at[slot(s, j)],
            send_sem=fcs.at[s],
            recv_sem=fcr.at[s],
            device_id={"inner": 1 - i},
        )

    def h_copy(s):
        return pltpu.make_async_remote_copy(
            src_ref=hbuf.at[slot(s, 1 - i)],
            dst_ref=sib.at[block(s)],
            send_sem=hs.at[s],
            recv_sem=hr.at[s],
            device_id={"inner": 1 - i},
        )

    def r_copy(s):
        return pltpu.make_async_remote_copy(
            src_ref=hbuf.at[slot(s, i)],
            dst_ref=ret.at[block(s)],
            send_sem=rs.at[s],
            recv_sem=rr.at[s],
            device_id={"egroup": partner(s)},
        )

    pairs = 2 * tok
    ids = ids_ref[...]
    ids_col = jnp.concatenate([ids[:, 0:1], ids[:, 1:2]], axis=0)
    qr = lax.broadcasted_iota(jnp.int32, (pairs, pairs), 0)
    qc = lax.broadcasted_iota(jnp.int32, (pairs, pairs), 1)
    order_r = jnp.where(qr >= tok, 2 * (qr - tok) + 1, 2 * qr)
    order_c = jnp.where(qc >= tok, 2 * (qc - tok) + 1, 2 * qc)
    ids_row = jnp.sum(jnp.where(qr == qc, ids_col.astype(F32), 0.0), axis=0, keepdims=True)
    ids_row = ids_row.astype(jnp.int32)
    same = ids_row == ids_col
    one, zero = jnp.float32(1), jnp.float32(0)
    slot_row = jnp.sum(jnp.where(same & (order_r < order_c), one, zero), axis=0, keepdims=True)
    slot_col = jnp.sum(jnp.where(same & (order_c < order_r), one, zero), axis=1, keepdims=True)

    def place(ids, slots):
        step = jnp.zeros(ids.shape, F32)
        for s in range(n):
            step = jnp.where(ids == partner(s), jnp.float32(s), step)
        return step * capp + slots

    to_row = place(ids_row, slot_row)
    to_col = place(ids_col, slot_col)
    position = lax.broadcasted_iota(jnp.int32, (rows, pairs), 0).astype(F32)
    hot = jnp.where(position == to_row, one, zero)
    sel[...] = (hot[:, :tok] + hot[:, tok:]).astype(BF16)
    gates = gates_ref[...].astype(F32)
    gates = jnp.concatenate([gates[:, 0:1], gates[:, 1:2]], axis=0)
    gates = jnp.broadcast_to(gates, (pairs, LANES)).astype(BF16)
    gate_sel[...] = jnp.dot(hot.astype(BF16), gates, preferred_element_type=F32).astype(BF16)

    pl.semaphore_wait(bar, n)

    def fill(s, src, dst, where):
        picks = sel[block(s), :]

        def tile(t, c):
            cols = pl.ds(pl.multiple_of(t * TILE, TILE), TILE)
            dst[where, cols] = jnp.dot(
                picks, src[:, cols], preferred_element_type=F32
            ).astype(BF16)
            return c

        lax.fori_loop(0, tiles, tile, 0)

    def start_x(s, c):
        fill(s, x_ref, snd_x, block(s))
        snd_x[block(s), dm:] = gate_sel[block(s), :]
        x_copy(s).start()
        return c

    lax.fori_loop(1, n, start_x, 0)
    fill(0, x_ref, rx, slot(0, i))
    rx[slot(0, i), dm:] = gate_sel[block(0), :]
    fx_copy(0, i).start()

    def fill_c(s, c):
        fill(s, cot_ref, snd_c, block(s))
        return c

    lax.fori_loop(1, n, fill_c, 0)
    fill(0, cot_ref, rc, slot(0, i))
    fc_copy(0, i).start()

    for copy in w_copies:
        copy.wait()

    def up_terms(s):
        fx_copy(s, 1 - i).wait_recv()
        inp = rx[chunk(s), :dm]
        pg[chunk(s), :] = jnp.dot(inp, wg[...], preferred_element_type=F32)
        pu[chunk(s), :] = jnp.dot(inp, wu[...], preferred_element_type=F32)

    up_terms(0)

    def phase_x(s, c):
        x_copy(s).wait_recv()
        fx_copy(s, i).start()
        c_copy(s).start()

        @pl.when(s > 1)
        def _():
            up_terms(s - 1)

        return c

    lax.fori_loop(1, n, phase_x, 0)
    up_terms(n - 1)

    def down_terms(s):
        fc_copy(s, 1 - i).wait_recv()
        back = nt_dot(rc[chunk(s), :], wd[...])
        gate_col = rx[chunk(s), dm : dm + 1].astype(F32)
        pre_gate, pre_up = pg[chunk(s), :], pu[chunk(s), :]
        logistic = 1.0 / (1.0 + jnp.exp(-pre_gate))
        active = pre_gate * logistic
        hidden = (active * pre_up).astype(BF16)
        scaled = gate_col * back
        d_gate = (scaled * pre_up * logistic * (1.0 + pre_gate * (1.0 - logistic))).astype(BF16)
        d_up = (scaled * active).astype(BF16)
        act[chunk(s), :] = hidden
        gpg[chunk(s), :] = d_gate
        gpu[chunk(s), :] = d_up
        mix = jnp.sum(hidden.astype(F32) * back, axis=1, keepdims=True)
        hbuf[chunk(s), dm:] = jnp.broadcast_to(mix, (pair, LANES)).astype(BF16)

        def tile(t, c):
            cols = pl.ds(pl.multiple_of(t * TILE, TILE), TILE)
            hbuf[chunk(s), cols] = (
                nt_dot(gpg[chunk(s), :], wg[cols, :]) + nt_dot(gpu[chunk(s), :], wu[cols, :])
            ).astype(BF16)
            return c

        lax.fori_loop(0, tiles, tile, 0)
        h_copy(s).start()

    def add_halves(s):
        h_copy(s).wait_recv()
        return (hbuf[slot(s, i), :].astype(F32) + sib[block(s), :].astype(F32)).astype(BF16)

    def give_back(s):
        hbuf[slot(s, i), :] = add_halves(s)
        r_copy(s).start()

    down_terms(0)

    def phase_c(s, c):
        c_copy(s).wait_recv()
        fc_copy(s, i).start()

        @pl.when(s > 1)
        def _():
            give_back(s - 1)

        down_terms(s)
        return c

    lax.fori_loop(1, n, phase_c, 0)
    give_back(n - 1)
    ret[block(0), :] = add_halves(0)

    def out_copies(t):
        cols = pl.ds(pl.multiple_of(t * TILE, TILE), TILE)
        return (
            pltpu.make_async_copy(wg.at[cols], gwg_hbm.at[cols], o_sem.at[0, t]),
            pltpu.make_async_copy(wu.at[cols], gwu_hbm.at[cols], o_sem.at[1, t]),
            pltpu.make_async_copy(wd.at[:, cols], gwd_hbm.at[:, cols], o_sem.at[2, t]),
        )

    def weight_grads(t, c):
        cols = pl.ds(pl.multiple_of(t * TILE, TILE), TILE)
        inp = rx[:, cols]
        wg[cols, :] = tn_dot(inp, gpg[...]).astype(BF16)
        wu[cols, :] = tn_dot(inp, gpu[...]).astype(BF16)
        gate_col = rx[:, dm : dm + 1].astype(F32)
        weighted = (gate_col * rc[:, cols].astype(F32)).astype(BF16)
        wd[:, cols] = tn_dot(act[...], weighted).astype(BF16)
        for copy in out_copies(t):
            copy.start()
        return c

    lax.fori_loop(0, tiles, weight_grads, 0)

    def finish(s, c):
        r_copy(s).wait_recv()
        return c

    lax.fori_loop(1, n, finish, 0)
    place_lane = lax.broadcasted_iota(jnp.int32, (pairs, rows), 1).astype(F32)
    hot_t = jnp.where(place_lane == to_col, one, zero)
    mixed = jnp.dot(hot_t.astype(BF16), ret[:, dm:], preferred_element_type=F32)
    gg_ref[...] = jnp.concatenate([mixed[:tok, 0:1], mixed[tok:, 0:1]], axis=1).astype(BF16)
    sel_t = (hot_t[:tok, :] + hot_t[tok:, :]).astype(BF16)
    for t in range(tiles):
        cols = slice(t * TILE, (t + 1) * TILE)
        gx_ref[:, cols] = jnp.dot(sel_t, ret[:, cols], preferred_element_type=F32).astype(BF16)

    def drain(s, c):
        x_copy(s).wait_send()
        c_copy(s).wait_send()
        r_copy(s).wait_send()
        return c

    lax.fori_loop(1, n, drain, 0)

    def drain_pairs(s, c):
        fx_copy(s, i).wait_send()
        fc_copy(s, i).wait_send()
        h_copy(s).wait_send()
        return c

    lax.fori_loop(0, n, drain_pairs, 0)

    def drain_out(t, c):
        for copy in out_copies(t):
            copy.wait()
        return c

    lax.fori_loop(0, tiles, drain_out, 0)


def shards(hidden_in, grad_out, gate_values, expert_ids, w_gate, w_up, w_down):
    tok, dm = hidden_in.shape
    per_token = expert_ids.shape[1]
    n = lax.axis_size("egroup")
    hid = w_gate.shape[2]
    capacity = tok * per_token * 3 // (2 * n)
    capp = -(-capacity // 16) * 16
    rows = n * capp
    wide = dm + LANES
    dma = pltpu.SemaphoreType.DMA
    vmem = pl.BlockSpec(memory_space=pltpu.VMEM)
    hbm = pl.BlockSpec(memory_space=pl.ANY)
    flops = 2 * 8 * 2 * rows * dm * hid
    gx, gg, gwg, gwu, gwd = pl.pallas_call(
        functools.partial(layer_kernel, n, capp),
        out_shape=(
            jax.ShapeDtypeStruct((tok, dm), BF16),
            jax.ShapeDtypeStruct((tok, per_token), BF16),
            jax.ShapeDtypeStruct((dm, hid), BF16),
            jax.ShapeDtypeStruct((dm, hid), BF16),
            jax.ShapeDtypeStruct((hid, dm), BF16),
        ),
        in_specs=[vmem] * 4 + [hbm] * 3,
        out_specs=(vmem, vmem, hbm, hbm, hbm),
        scratch_shapes=[
            pltpu.VMEM((dm, hid), BF16),
            pltpu.VMEM((dm, hid), BF16),
            pltpu.VMEM((hid, dm), BF16),
            pltpu.VMEM((rows, tok), BF16),
            pltpu.VMEM((rows, LANES), BF16),
            pltpu.VMEM((rows, wide), BF16),
            pltpu.VMEM((rows, dm), BF16),
            pltpu.VMEM((2 * rows, wide), BF16),
            pltpu.VMEM((2 * rows, dm), BF16),
            pltpu.VMEM((2 * rows, hid), F32),
            pltpu.VMEM((2 * rows, hid), F32),
            pltpu.VMEM((2 * rows, hid), BF16),
            pltpu.VMEM((2 * rows, hid), BF16),
            pltpu.VMEM((2 * rows, hid), BF16),
            pltpu.VMEM((2 * rows, wide), BF16),
            pltpu.VMEM((rows, wide), BF16),
            pltpu.VMEM((rows, wide), BF16),
            dma((3,)),
            dma((3, dm // TILE)),
        ]
        + [dma((n,))] * 12,
        compiler_params=pltpu.CompilerParams(
            collective_id=0,
            has_side_effects=True,
            vmem_limit_bytes=63 * 1024 * 1024,
        ),
        cost_estimate=pl.CostEstimate(
            flops=flops, bytes_accessed=30_000_000, transcendentals=2 * rows * hid
        ),
        name="expert_layer",
    )(
        hidden_in,
        grad_out,
        gate_values,
        expert_ids,
        w_gate[0],
        w_up[0],
        w_down[0],
    )
    return gx, gg, gwg[None], gwu[None], gwd[None]


def solution(mesh):
    in_specs = (
        P(("parts", "egroup", "inner"), None),
        P(("parts", "egroup", "inner"), None),
        P(("parts", "egroup", "inner"), None),
        P(("parts", "egroup", "inner"), None),
        P("egroup", None, "inner"),
        P("egroup", None, "inner"),
        P("egroup", "inner", None),
    )
    out_specs = (
        P(("parts", "egroup", "inner"), None),
        P(("parts", "egroup", "inner"), None),
        P(("parts", "egroup"), None, "inner"),
        P(("parts", "egroup"), None, "inner"),
        P(("parts", "egroup"), "inner", None),
    )
    return jax.shard_map(shards, mesh=mesh, in_specs=in_specs, out_specs=out_specs, check_vma=False)
```
